32 devices in a mesh: gx: 8 (over y, x, core), gy: 4 (over z).
Axes of the slice: x: 2, y: 2, z: 4, core: 2. Of those that a mesh axis runs over, the one named last changes fastest.
Arguments:
- nest_fields: float32 [5, 80, 24, 1536], P(None, None, 'gx', 'gy'), may hold values from -6 to 6
- boundary_strip: float32 [8, 5, 80, 1536], P('gx', None, None, 'gy'), may hold values from -6 to 6
- strip_owner: int32 [4], replicated, may hold values from 0 to 7, as said below
- terrain_slope: float32 [24, 1536], P('gx', 'gy'), may hold values from -0.6 to 0.6
- column_metric: float32 [24, 1536], P('gx', 'gy'), may hold values from 0.6 to 1.6
- relax_rate: float32 [24, 1536], P('gx', 'gy'), may hold values from 0.05 to 2
- parent_state: float32 [8, 512, 320], P('gx', 'gy'), may hold values from -6 to 6
- intersection_cell: int32 [8, 4, 4, 4], P('gx', 'gy'), may hold values from 0 to 127
- intersection_row: int32 [8, 4, 4, 4], P('gx', 'gy'), may hold values from 0 to 127
- intersection_count: int32 [8, 4, 4], P('gx', 'gy'), may hold values from 1 to 4, as said below
Outputs:
- nest_out: float32 [5, 80, 24, 1536], P(None, None, 'gx', 'gy')
- parent_out: float32 [8, 512, 320], P('gx', 'gy')
The draws below stay inside these ranges and needn't reach their ends.
Inputs may be any that keep to these rules, and one draw needn't show every extreme that they name: `strip_owner`: x index that holds the boundary rows of each y block; both 0 and 7 occur. `intersection_count`: at most 4 records go from one device to one y index; in each x group one y index receives 4 records from every device of the group.
All inputs are finite; a program needn't handle non-finite values.
Results may differ from the reference program's by a relative error of at most 0.0003.
Values sent between devices are 32-bit elements; how exact they have to be, the bound alone decides.
A program may use at most 128 MiB of HBM per device.

```python
import math
import jax
import jax.numpy as jnp
from jax import lax

CX = 3
CY = 384
NZ = 80
CAP = 4
NX = 24
NY = 1536
PCELL = 128
PARENT_ROWS = 512
FEAT = 320
N_GX = 8
N_GY = 4


def draw_strip_owner(key, part):
    first, second = jax.random.split(key)
    picks = jax.random.randint(first, (N_GY,), 0, N_GX)
    order = jax.random.permutation(second, N_GY)
    picks = jnp.where(order == 0, N_GX - 1, picks)
    return jnp.where(order == 1, 0, picks).astype(jnp.int32)


def draw_intersection_count(key, part):
    first, second, third = jax.random.split(key, 3)
    left = jax.random.randint(first, (N_GX, N_GY, N_GY), 0, CAP + 1)
    right = jax.random.randint(second, (N_GX, N_GY, N_GY), 0, CAP + 1)
    counts = jnp.minimum(CAP, 1 + left * right // CAP)
    full_dest = jax.random.randint(third, (N_GX,), 0, N_GY)
    dest_ids = jnp.arange(N_GY)
    counts = jnp.where(dest_ids[None, None, :] == full_dest[:, None, None], CAP, counts)
    return counts.astype(jnp.int32)


def set_ends(result, key, low, top_value):
    dims = result.shape
    place = [jax.random.randint(jax.random.fold_in(key, axis), (), 0, dims[axis]) for axis in range(len(dims))]
    result = result.at[tuple(place)].set(low)
    longest = dims.index(max(dims))
    place[longest] = (place[longest] + 1) % dims[longest]
    return result.at[tuple(place)].set(top_value)


def block_levels(own_key, extent, cuts, smallest, top_value):
    loudness, own = 1.0, jax.random.fold_in(own_key, 6)
    for position, blocks in cuts:
        heights = jnp.exp(jax.random.uniform(jax.random.fold_in(own, position), (blocks,), jnp.float32, smallest / len(cuts), top_value / len(cuts)))
        loudness = loudness * jnp.repeat(heights, extent[position] // blocks).reshape([-1 if axis == position else 1 for axis in range(len(extent))])
    return loudness


def scatter_about(rng, dims, width, most, pieces=(), held_as=jnp.bfloat16):
    gain = block_levels(rng, dims, pieces, -0.22, 0.18) if pieces else 1.0
    result = jax.random.normal(rng, dims, jnp.float32) * width * gain
    return jnp.minimum(jnp.maximum(result, -most), most).astype(held_as)


def setup_inputs(seed: int = 0) -> dict:
    keys = jax.random.split(jax.random.key(seed), 11)
    return {
        "nest_fields": scatter_about(keys[0], (5, NZ, NX, NY), 1.0, 6.0, ((2, 8), (3, 4)), jnp.float32),
        "boundary_strip": scatter_about(keys[1], (N_GX, 5, NZ, NY), 1.0, 6.0, ((0, 8), (3, 4)), jnp.float32),
        "strip_owner": draw_strip_owner(jax.random.fold_in(keys[10], 71), 0),
        "terrain_slope": jnp.clip(jax.random.uniform(keys[3], (NX, NY), jnp.float32, -0.6, 0.6) * block_levels(keys[3], (NX, NY), ((0, 8), (1, 4)), -0.4, 0.0), -0.6, 0.6),
        "column_metric": jnp.clip(jnp.exp(math.log(1.6) - 0.98082923 * jax.random.uniform(keys[4], (NX, NY), jnp.float32) ** block_levels(keys[4], (NX, NY), ((0, 8), (1, 4)), -0.2, 0.2)), 0.6, 1.6),
        "relax_rate": jnp.clip(jnp.exp(math.log(2.0) - 3.6888794 * jax.random.uniform(keys[5], (NX, NY), jnp.float32) ** block_levels(keys[5], (NX, NY), ((0, 8), (1, 4)), -0.2, 0.2)), 0.05, 2.0),
        "parent_state": scatter_about(keys[6], (N_GX, PARENT_ROWS, FEAT), 1.0, 6.0, ((0, 8), (1, 4)), jnp.float32),
        "intersection_cell": set_ends(jax.random.randint(keys[7], (N_GX, N_GY, N_GY, CAP), 0, PCELL), jax.random.fold_in(keys[7], 1), 0, PCELL - 1).astype(jnp.int32),
        "intersection_row": set_ends(jax.random.randint(keys[8], (N_GX, N_GY, N_GY, CAP), 0, PCELL), jax.random.fold_in(keys[8], 1), 0, PCELL - 1).astype(jnp.int32),
        "intersection_count": draw_intersection_count(jax.random.fold_in(keys[10], 71), 0),
    }


time_step = 0.25
sound_speed = 1.0
viscosity = 0.05
buoyancy = 0.5
wind_east = 0.6
wind_north = -0.4


def tendency(padded, slope, metric, relax, boundary):
    center = padded[:, :, 1:-1, 1:-1]
    east_cell = padded[:, :, 2:, 1:-1]
    west_cell = padded[:, :, :-2, 1:-1]
    north_cell = padded[:, :, 1:-1, 2:]
    south_cell = padded[:, :, 1:-1, :-2]
    vertical = jnp.pad(center, ((0, 0), (1, 1), (0, 0), (0, 0)))
    along_z = 0.5 * (vertical[:, 2:] - vertical[:, :-2]) * metric
    along_x = 0.5 * (east_cell - west_cell) - slope * along_z
    along_y = 0.5 * (north_cell - south_cell)
    spread = east_cell + west_cell + north_cell + south_cell - 4.0 * center
    common = -(wind_east * along_x + wind_north * along_y) + viscosity * spread + relax * (boundary[:, :, None, :] - center)
    tend_east = common[0] - sound_speed * along_x[4]
    tend_north = common[1] - sound_speed * along_y[4]
    tend_vert = common[2] - sound_speed * along_z[4] + buoyancy * center[3]
    tend_heat = common[3] - buoyancy * center[2]
    tend_press = common[4] - sound_speed * (along_x[0] + along_y[1] + along_z[2])
    return jnp.stack([tend_east, tend_north, tend_vert, tend_heat, tend_press])


def advance(initial, slope, metric, relax, boundary, inside):
    current = initial
    for weight in (1.0 / 3.0, 0.5, 1.0):
        padded = jnp.pad(current, ((0, 0), (0, 0), (1, 1), (1, 1)))
        current = (initial + (weight * time_step) * tendency(padded, slope, metric, relax, boundary)) * inside
    return current[:, :, 3:-3, 3:-3]


def reference(nest_fields, boundary_strip, strip_owner, terrain_slope, column_metric, relax_rate, parent_state, intersection_cell, intersection_row, intersection_count):
    y_owner = strip_owner[jnp.arange(NY) // CY]
    boundary = jnp.transpose(boundary_strip[y_owner, :, :, jnp.arange(NY)], (1, 2, 0))
    block_x = CX * math.gcd(N_GX, 8)
    block_y = CY * math.gcd(N_GY, 4)
    count_x = NX // block_x
    count_y = NY // block_y
    fields_pad = jnp.pad(nest_fields, ((0, 0), (0, 0), (3, 3), (3, 3)))
    coef_pad = jnp.pad(jnp.stack([terrain_slope, column_metric, relax_rate]), ((0, 0), (3, 3), (3, 3)))
    bound_pad = jnp.pad(boundary, ((0, 0), (0, 0), (3, 3)))
    inside_pad = jnp.pad(jnp.ones((NX, NY), nest_fields.dtype), 3)

    def one_block(number):
        corner_x = ((number // count_y) * block_x).astype(jnp.int32)
        corner_y = ((number % count_y) * block_y).astype(jnp.int32)
        anchor = jnp.int32(0)
        initial = lax.dynamic_slice(fields_pad, (anchor, anchor, corner_x, corner_y), (5, NZ, block_x + 6, block_y + 6))
        coefs = lax.dynamic_slice(coef_pad, (anchor, corner_x, corner_y), (3, block_x + 6, block_y + 6))
        bound_block = lax.dynamic_slice(bound_pad, (anchor, anchor, corner_y), (5, NZ, block_y + 6))
        inside = lax.dynamic_slice(inside_pad, (corner_x, corner_y), (block_x + 6, block_y + 6))
        return advance(initial, coefs[0], coefs[1], coefs[2], bound_block, inside)

    blocks = lax.map(one_block, jnp.arange(count_x * count_y, dtype=jnp.int32))
    nest_out = blocks.reshape(count_x, count_y, 5, NZ, block_x, block_y).transpose(2, 3, 0, 4, 1, 5).reshape(5, NZ, NX, NY)

    chosen = jnp.stack([nest_out[0], nest_out[1], nest_out[3], nest_out[4]])
    coarse = chosen.reshape(4, NZ, NX // 3, 3, NY // 3, 3).mean(axis=(3, 5))
    cells_dev = coarse.transpose(2, 3, 0, 1).reshape(N_GX, CX // 3, N_GY, CY // 3, FEAT)
    cells_dev = cells_dev.transpose(0, 2, 1, 3, 4).reshape(N_GX, N_GY, PCELL, FEAT)
    flat_cells = intersection_cell.reshape(N_GX, N_GY, N_GY * CAP)
    group_ids = jnp.arange(N_GX)[:, None, None]
    source_ids = jnp.arange(N_GY)[None, :, None]
    records = cells_dev[group_ids, source_ids, flat_cells]
    active = jnp.arange(CAP)[None, None, None, :] < intersection_count[..., None]
    group_col = jnp.arange(N_GX)[:, None, None, None]
    dest_col = jnp.arange(N_GY)[None, None, :, None]
    segment = jnp.where(active, group_col * PARENT_ROWS + dest_col * PCELL + intersection_row, N_GX * PARENT_ROWS).astype(jnp.int32)
    values = records.reshape(-1, FEAT)
    seg_flat = segment.reshape(-1)
    totals = jax.ops.segment_sum(values, seg_flat, num_segments=N_GX * PARENT_ROWS + 1)[:-1]
    tallies = jax.ops.segment_sum(jnp.ones(seg_flat.shape, values.dtype), seg_flat, num_segments=N_GX * PARENT_ROWS + 1)[:-1]
    flat_parent = parent_state.reshape(-1, FEAT)
    merged = jnp.where(tallies[:, None] > 0, totals / jnp.maximum(tallies, 1.0)[:, None], flat_parent)
    return nest_out, merged.reshape(N_GX, PARENT_ROWS, FEAT)
```

```python
import functools
import jax
import jax.numpy as jnp
from jax import lax
from jax.experimental import pallas as pl
from jax.experimental.pallas import tpu as pltpu
from jax.sharding import PartitionSpec as P

MESH = pl.DeviceIdType.MESH
time_step = 0.25
viscosity = 0.05
buoyancy = 0.5
wind_east = 0.6
wind_north = -0.4
PAD = 8
CH = 16
HIGH = lax.Precision.HIGHEST


def kernel(
    n_gx, n_gy, cap,
    owner_ref, cell_ref, row_ref, count_ref,
    nest_ref, strip_ref, slope_ref, metric_ref, relax_ref, parent_ref,
    out_ref, pout_ref,
    q, halo, edge_out, edge_in, coef,
    strip, got_half, half, got_quarter, quarter, got_other, whole_half, got_rest, bound,
    total, records, got_records,
    load_sem, strip_sem, x_send, x_recv, y_send, y_recv, b_send, b_recv, r_send, r_recv, out_sem,
):
    fields, levels, width = q.shape[1], q.shape[3] - 2 * PAD, q.shape[4]
    chunks = levels // CH
    gx, gy = lax.axis_index("gx"), lax.axis_index("gy")
    tile = width // 3
    inner = pl.ds(PAD, levels)

    load = pltpu.make_async_copy(nest_ref, q.at[0, :, :, inner, :], load_sem)
    load.start()
    load_strip = pltpu.make_async_copy(strip_ref, strip, strip_sem)
    load_strip.start()

    barrier = pltpu.get_barrier_semaphore()
    for off in range(1, n_gx):
        pl.semaphore_signal(barrier, inc=1, device_id={"gx": lax.rem(gx + off, n_gx)}, device_id_type=MESH)
    for off in range(1, n_gy):
        pl.semaphore_signal(barrier, inc=1, device_id={"gy": lax.rem(gy + off, n_gy)}, device_id_type=MESH)

    zero = jnp.zeros((PAD, width), jnp.float32)

    def clear(s, _):
        for f in range(fields):
            for x in range(3):
                q[s, f, x, 0:PAD, :] = zero
                q[s, f, x, PAD + levels :, :] = zero
        return 0

    lax.fori_loop(0, 3, clear, 0)

    def clear_side(side):
        def body(i, _):
            for f in range(fields):
                halo[side, i // (levels // 8), f, pl.ds(pl.multiple_of(i % (levels // 8) * 8, 8), 8), :] = zero
            return 0

        lax.fori_loop(0, 3 * levels // 8, body, 0)

    @pl.when(gx == 0)
    def _():
        clear_side(0)

    @pl.when(gx == n_gx - 1)
    def _():
        clear_side(1)

    @pl.when(gy == 0)
    def _():
        edge_in[0] = jnp.zeros(edge_in.shape[1:], jnp.float32)

    @pl.when(gy == n_gy - 1)
    def _():
        edge_in[1] = jnp.zeros(edge_in.shape[1:], jnp.float32)

    for x in range(3):
        for i, ref in enumerate((slope_ref, metric_ref, relax_ref)):
            coef[i, x] = jnp.broadcast_to(ref[x : x + 1, :], (8, width))

    has_low = (gx > 0, gy > 0)
    has_high = (gx < n_gx - 1, gy < n_gy - 1)

    def x_copy(side, s, k):
        rows = pl.ds(pl.multiple_of(k * CH, 8), CH)
        padded = pl.ds(pl.multiple_of(k * CH + PAD, 8), CH)
        peer = gx + 1 if side == 0 else gx - 1
        return pltpu.make_async_remote_copy(
            src_ref=q.at[s, :, 2 if side == 0 else 0, padded, :],
            dst_ref=halo.at[side, s, :, rows, :],
            send_sem=x_send.at[side, s, k],
            recv_sem=x_recv.at[side, s, k],
            device_id={"gx": peer},
            device_id_type=MESH,
        )

    def y_copy(side, s, k):
        rows = pl.ds(pl.multiple_of(k * CH, 8), CH)
        peer = gy + 1 if side == 0 else gy - 1
        return pltpu.make_async_remote_copy(
            src_ref=edge_out.at[side, s, rows, :],
            dst_ref=edge_in.at[side, s, rows, :],
            send_sem=y_send.at[side, s, k],
            recv_sem=y_recv.at[side, s, k],
            device_id={"gy": peer},
            device_id_type=MESH,
        )

    def send(copy, s, k, axis):
        @pl.when(has_high[axis])
        def _():
            copy(0, s, k).start()

        @pl.when(has_low[axis])
        def _():
            copy(1, s, k).start()

    def received(copy, s, k, axis):
        @pl.when(has_low[axis])
        def _():
            copy(0, s, k).wait_recv()

        @pl.when(has_high[axis])
        def _():
            copy(1, s, k).wait_recv()

    def sent(copy, s, k, axis):
        @pl.when(has_high[axis])
        def _():
            copy(0, s, k).wait_send()

        @pl.when(has_low[axis])
        def _():
            copy(1, s, k).wait_send()

    lane = lax.broadcasted_iota(jnp.int32, (CH, tile), 1)

    def pack(s, k):
        rows = pl.ds(pl.multiple_of(k * CH + PAD, 8), CH)
        high = jnp.zeros((CH, tile), jnp.float32)
        low = jnp.zeros((CH, tile), jnp.float32)
        for f in range(fields):
            for x in range(3):
                j = f * 3 + x
                last = q[s, f, x, rows, width - tile : width]
                first = q[s, f, x, rows, 0:tile]
                high = jnp.where(lane == j, pltpu.roll(last, j + 1, 1), high)
                low = jnp.where(lane == j, pltpu.roll(first, j, 1) if j else first, low)
        flat = pl.ds(pl.multiple_of(k * CH, 8), CH)
        edge_out[0, s, flat, :] = high
        edge_out[1, s, flat, :] = low

    pl.semaphore_wait(barrier, n_gx - 1 + n_gy - 1)
    load_strip.wait()

    owner = owner_ref[gy]
    n_rows, n_half, n_quarter = bound.shape[0], half.shape[0], half.shape[0] // 2
    core = lax.rem(gx, 2)
    far = n_gx // 2
    part = lax.rem(gx // far, 2)

    def flip(bit):
        digit = lax.rem(gx // bit, 2)
        return gx + bit - 2 * bit * digit

    def differs(bit):
        return lax.rem(gx // bit, 2) != lax.rem(owner // bit, 2)

    def b_copy(src, dst, number, bit):
        return pltpu.make_async_remote_copy(
            src_ref=src, dst_ref=dst, send_sem=b_send.at[number], recv_sem=b_recv.at[number],
            device_id={"gx": flip(bit)}, device_id_type=MESH,
        )

    def half_at(c):
        return pl.ds(pl.multiple_of(c * (n_rows - n_half), 8), n_half)

    def quarter_at(c):
        return pl.ds(pl.multiple_of(c * n_quarter, 8), n_quarter)

    step0 = b_copy(strip.at[half_at(1 - core), :], got_half, 0, 1)
    step0.start()
    load.wait()

    def first_sends(k, _):
        send(x_copy, 0, k, 0)
        return 0

    lax.fori_loop(0, chunks, first_sends, 0)
    step0.wait_recv()
    half[...] = jnp.where(differs(1), got_half[...], strip[half_at(core), :])
    step1 = b_copy(half.at[quarter_at(1 - part), :], got_quarter, 1, far)
    step1.start()

    def first_edges(k, _):
        pack(0, k)
        send(y_copy, 0, k, 1)
        return 0

    lax.fori_loop(0, chunks, first_edges, 0)
    step1.wait_recv()
    quarter[0] = jnp.where(differs(far), got_quarter[...], half[quarter_at(part), :])
    pending = [step0, step1]
    bit, i = 2, 0
    while bit < far:
        step = b_copy(quarter.at[i], got_other.at[i], 2 + i, bit)
        step.start()
        step.wait_recv()
        quarter[i + 1] = jnp.where(differs(bit), got_other[i], quarter[i])
        pending.append(step)
        bit, i = bit * 2, i + 1
    whole_half[quarter_at(part), :] = quarter[i]
    step = b_copy(quarter.at[i], whole_half.at[quarter_at(part), :], 2 + i, far)
    step.start()
    step.wait_recv()
    pending.append(step)
    step = b_copy(whole_half, got_rest, 3 + i, 1)
    step.start()
    bound[half_at(core), :] = whole_half[...]
    step.wait_recv()
    pending.append(step)
    bound[half_at(1 - core), :] = got_rest[...]

    wide_lane = lax.broadcasted_iota(jnp.int32, (8, width), 1)
    level = lax.broadcasted_iota(jnp.int32, (8, width), 0)
    is_bottom, is_top = level == 0, level == 7
    is_first, is_last = wide_lane == 0, wide_lane == width - 1

    def block(s, z0, x, weight):
        slope, metric, relax = coef[0, x], coef[1, x], coef[2, x]
        rows = pl.ds(pl.multiple_of(z0 + PAD, 8), 8)
        flat = pl.ds(pl.multiple_of(z0, 8), 8)
        from_south, from_north = edge_in[0, s, flat, :], edge_in[1, s, flat, :]
        centers, axs, ays, azs, commons = [], [], [], [], []
        for f in range(fields):
            c = q[s, f, x, rows, :]
            above = q[s, f, x, pl.ds(pl.multiple_of(z0 + PAD + 8, 8), 8), :]
            below = q[s, f, x, pl.ds(pl.multiple_of(z0 + PAD - 8, 8), 8), :]
            up = pltpu.roll(jnp.where(is_bottom, above, c), 7, 0)
            down = pltpu.roll(jnp.where(is_top, below, c), 1, 0)
            east = q[s, f, x + 1, rows, :] if x < 2 else halo[1, s, f, flat, :]
            west = q[s, f, x - 1, rows, :] if x > 0 else halo[0, s, f, flat, :]
            j = f * 3 + x
            a = pltpu.roll(from_south, tile - j, 1) if j else from_south
            b = pltpu.roll(from_north, tile - 1 - j, 1)
            south = jnp.where(is_first, jnp.concatenate([a] * 3, axis=1), pltpu.roll(c, 1, 1))
            north = jnp.where(is_last, jnp.concatenate([b] * 3, axis=1), pltpu.roll(c, width - 1, 1))
            az = (0.5 * (up - down)) * metric
            ax = 0.5 * (east - west) - slope * az
            ay = 0.5 * (north - south)
            spread = (east + west) + (north + south) - 4.0 * c
            limit = bound[pl.ds(pl.multiple_of(f * levels + z0, 8), 8), :]
            common = relax * (limit - c) + viscosity * spread - (wind_east * ax + wind_north * ay)
            centers.append(c)
            axs.append(ax)
            ays.append(ay)
            azs.append(az)
            commons.append(common)
        tend = [
            commons[0] - axs[4],
            commons[1] - ays[4],
            commons[2] - azs[4] + buoyancy * centers[3],
            commons[3] - buoyancy * centers[2],
            commons[4] - (axs[0] + ays[1] + azs[2]),
        ]
        for f in range(fields):
            q[s + 1, f, x, rows, :] = q[0, f, x, rows, :] + weight * tend[f]

    def out_copy(k):
        rows = pl.ds(pl.multiple_of(k * CH, 8), CH)
        padded = pl.ds(pl.multiple_of(k * CH + PAD, 8), CH)
        return pltpu.make_async_copy(q.at[3, :, :, padded, :], out_ref.at[:, :, rows, :], out_sem.at[k])

    def substep(s, _):
        weight = time_step * jnp.where(s == 0, 1.0 / 3.0, jnp.where(s == 1, 0.5, 1.0)).astype(jnp.float32)

        def chunk(k, _):
            received(y_copy, s, k, 1)
            received(x_copy, s, k, 0)

            def rows8(i, _):
                for x in (0, 2, 1):
                    block(s, k * CH + i * 8, x, weight)
                return 0

            lax.fori_loop(0, CH // 8, rows8, 0)

            @pl.when(s < 2)
            def _():
                send(x_copy, s + 1, k, 0)
                pack(s + 1, k)
                send(y_copy, s + 1, k, 1)

            @pl.when(s == 2)
            def _():
                out_copy(k).start()

            return 0

        lax.fori_loop(0, chunks, chunk, 0)
        return 0

    lax.fori_loop(0, 3, substep, 0)

    feat = 4 * levels
    total[feat:, :] = jnp.zeros((total.shape[0] - feat, width), jnp.float32)
    for i, f in enumerate((0, 1, 3, 4)):
        total[i * levels : (i + 1) * levels, :] = q[3, f, 0, inner, :] + q[3, f, 1, inner, :] + q[3, f, 2, inner, :]
    sub = lax.broadcasted_iota(jnp.int32, (8, width), 0)
    picks, targets = [], []
    for d in range(n_gy):
        pick = jnp.zeros((8, width), jnp.float32)
        target = jnp.full((8, width), -1, jnp.int32)
        for slot in range(cap):
            live = jnp.where(count_ref[d] > slot, slot, -1)
            shifted = wide_lane - 3 * cell_ref[d * cap + slot]
            here = sub == live
            pick = jnp.where(here & (shifted >= 0) & (shifted < 3), 1.0, pick)
            target = jnp.where(here, row_ref[d * cap + slot], target)
        picks.append(pick)
        targets.append(target.astype(jnp.float32))
    pick = jnp.concatenate(picks, axis=0)
    target = jnp.concatenate(targets, axis=0)
    sums = lax.dot_general(
        pick, total[...], (((1,), (1,)), ((), ())), precision=HIGH, preferred_element_type=jnp.float32
    )
    column = lax.broadcasted_iota(jnp.int32, sums.shape, 1)
    records[...] = jnp.where(column == feat, target[:, :1], sums * (1.0 / 9.0))

    def r_copy(off):
        peer = lax.rem(gy + off, n_gy)
        return pltpu.make_async_remote_copy(
            src_ref=records.at[pl.ds(pl.multiple_of(peer * 8, 8), 8), :],
            dst_ref=got_records.at[pl.ds(pl.multiple_of(gy * 8, 8), 8), :],
            send_sem=r_send.at[off - 1],
            recv_sem=r_recv.at[off - 1],
            device_id={"gy": peer},
            device_id_type=MESH,
        )

    for off in range(1, n_gy):
        r_copy(off).start()
    mine = pl.ds(pl.multiple_of(gy * 8, 8), 8)
    got_records[mine, :] = records[mine, :]
    for step in pending:
        step.wait_send()

    def settle(s, _):
        def inner_settle(k, _):
            sent(x_copy, s, k, 0)
            sent(y_copy, s, k, 1)
            return 0

        lax.fori_loop(0, chunks, inner_settle, 0)
        return 0

    lax.fori_loop(0, 3, settle, 0)
    for off in range(1, n_gy):
        r_copy(off).wait()
    got = got_records[...]
    parents = lax.broadcasted_iota(jnp.int32, (got.shape[0], parent_ref.shape[1]), 1).astype(jnp.float32)
    onehot = jnp.where(got[:, feat : feat + 1] == parents, 1.0, 0.0)
    totals = lax.dot_general(
        got, onehot, (((0,), (0,)), ((), ())), precision=HIGH, preferred_element_type=jnp.float32
    )
    tally = jnp.sum(onehot, axis=0, keepdims=True)
    pout_ref[...] = jnp.where(tally > 0, totals[:feat] / jnp.maximum(tally, 1.0), parent_ref[...])

    def settle_out(k, _):
        out_copy(k).wait()
        return 0

    lax.fori_loop(0, chunks, settle_out, 0)


def on_device(
    n_gx, n_gy,
    nest_fields, boundary_strip, strip_owner, terrain_slope, column_metric, relax_rate,
    parent_state, intersection_cell, intersection_row, intersection_count,
):
    fields, levels, cells_x, width = nest_fields.shape
    cap = intersection_cell.shape[3]
    chunks = levels // CH
    n_rows = fields * levels
    n_quarter = -(-n_rows // 32) * 8
    n_half = 2 * n_quarter
    bits = max(n_gx.bit_length() - 3, 1)
    feat = 4 * levels
    feat_pad = -(-(feat + 1) // 128) * 128
    tile = width // 3
    f32 = jnp.float32
    smem = pl.BlockSpec(memory_space=pltpu.SMEM)
    vmem = pl.BlockSpec(memory_space=pltpu.VMEM)
    hbm = pl.BlockSpec(memory_space=pl.ANY)
    dma = pltpu.SemaphoreType.DMA
    out, parent = pl.pallas_call(
        functools.partial(kernel, n_gx, n_gy, cap),
        out_shape=(
            jax.ShapeDtypeStruct((fields, cells_x, levels, width), f32),
            jax.ShapeDtypeStruct((feat, parent_state.shape[1]), f32),
        ),
        in_specs=[smem] * 4 + [hbm] * 2 + [vmem] * 4,
        out_specs=(hbm, vmem),
        scratch_shapes=[
            pltpu.VMEM((4, fields, 3, levels + 2 * PAD, width), f32),
            pltpu.VMEM((2, 3, fields, levels, width), f32),
            pltpu.VMEM((2, 3, levels, tile), f32),
            pltpu.VMEM((2, 3, levels, tile), f32),
            pltpu.VMEM((3, 3, 8, width), f32),
            pltpu.VMEM((n_rows, width), f32),
            pltpu.VMEM((n_half, width), f32),
            pltpu.VMEM((n_half, width), f32),
            pltpu.VMEM((n_quarter, width), f32),
            pltpu.VMEM((bits + 1, n_quarter, width), f32),
            pltpu.VMEM((bits, n_quarter, width), f32),
            pltpu.VMEM((n_half, width), f32),
            pltpu.VMEM((n_half, width), f32),
            pltpu.VMEM((n_rows, width), f32),
            pltpu.VMEM((feat_pad, width), f32),
            pltpu.VMEM((n_gy * 8, feat_pad), f32),
            pltpu.VMEM((n_gy * 8, feat_pad), f32),
            dma,
            dma,
            dma((2, 3, chunks)),
            dma((2, 3, chunks)),
            dma((2, 3, chunks)),
            dma((2, 3, chunks)),
            dma((bits + 4,)),
            dma((bits + 4,)),
            dma((n_gy,)),
            dma((n_gy,)),
            dma((chunks,)),
        ],
        compiler_params=pltpu.CompilerParams(
            collective_id=0, has_side_effects=True, vmem_limit_bytes=40 * 1024 * 1024
        ),
    )(
        strip_owner,
        intersection_cell.reshape(-1),
        intersection_row.reshape(-1),
        intersection_count.reshape(-1),
        nest_fields.transpose(0, 2, 1, 3),
        boundary_strip.reshape(n_rows, width),
        terrain_slope,
        column_metric,
        relax_rate,
        parent_state[0].T,
    )
    return out.transpose(0, 2, 1, 3), parent.T[None]


def solution(mesh):
    placed = (
        P(None, None, "gx", "gy"),
        P("gx", None, None, "gy"),
        P(),
        P("gx", "gy"),
        P("gx", "gy"),
        P("gx", "gy"),
        P("gx", "gy", None),
        P("gx", "gy", None, None),
        P("gx", "gy", None, None),
        P("gx", "gy", None),
    )
    return jax.shard_map(
        functools.partial(on_device, mesh.shape["gx"], mesh.shape["gy"]),
        mesh=mesh,
        in_specs=placed,
        out_specs=(P(None, None, "gx", "gy"), P("gx", "gy", None)),
        check_vma=False,
    )
```

```python
import functools
import jax
import jax.numpy as jnp
from jax import lax
from jax.experimental import pallas as pl
from jax.experimental.pallas import tpu as pltpu
from jax.sharding import PartitionSpec as P

MESH = pl.DeviceIdType.MESH
time_step = 0.25
viscosity = 0.05
buoyancy = 0.5
wind_east = 0.6
wind_north = -0.4
PAD = 8
CH = 16
PIECES = 2
HIGH = lax.Precision.HIGHEST


def kernel(
    n_gx, n_gy, cap, pieces,
    owner_ref, cell_ref, row_ref, count_ref,
    nest_ref, strip_ref, slope_hbm, metric_hbm, relax_hbm, parent_hbm,
    out_ref, pout_ref,
    q, halo, edge_out, edge_in, coef,
    strip, got_half, half, got_quarter, quarter, got_other, whole_half, got_rest, bound,
    total, records, got_records, maps, parent_ref,
    load_sem, strip_sem, x_send, x_recv, y_send, y_recv, b_send, b_recv, r_send, r_recv, out_sem, small_sem,
    passing, pass_send, pass_recv,
):
    fields, levels, width = q.shape[1], q.shape[3] - 2 * PAD, q.shape[4]
    chunks = levels // CH
    gx, gy = lax.axis_index("gx"), lax.axis_index("gy")
    tile = width // 3
    inner = pl.ds(PAD, levels)
    far = n_gx // 2

    load = pltpu.make_async_copy(nest_ref, q.at[0, :, :, inner, :], load_sem)
    load.start()
    load_strip = pltpu.make_async_copy(strip_ref, strip, strip_sem)
    load_strip.start()
    load_maps = [
        pltpu.make_async_copy(ref, maps.at[i], small_sem.at[i])
        for i, ref in enumerate((slope_hbm, metric_hbm, relax_hbm))
    ]
    for copy in load_maps:
        copy.start()
    load_parent = pltpu.make_async_copy(parent_hbm, parent_ref, small_sem.at[3])
    load_parent.start()

    barrier = pltpu.get_barrier_semaphore()
    for off in range(1, n_gx):
        pl.semaphore_signal(barrier, inc=1, device_id={"gx": lax.rem(gx + off, n_gx)}, device_id_type=MESH)
    for off in range(1, n_gy):
        pl.semaphore_signal(barrier, inc=1, device_id={"gy": lax.rem(gy + off, n_gy)}, device_id_type=MESH)

    zero = jnp.zeros((PAD, width), jnp.float32)

    def clear(s, _):
        for f in range(fields):
            for x in range(3):
                q[s, f, x, 0:PAD, :] = zero
                q[s, f, x, PAD + levels :, :] = zero
        return 0

    lax.fori_loop(0, 3, clear, 0)

    def clear_side(side):
        def body(i, _):
            for f in range(fields):
                halo[side, i // (levels // 8), f, pl.ds(pl.multiple_of(i % (levels // 8) * 8, 8), 8), :] = zero
            return 0

        lax.fori_loop(0, 3 * levels // 8, body, 0)

    @pl.when(gx == 0)
    def _():
        clear_side(0)

    @pl.when(gx == n_gx - 1)
    def _():
        clear_side(1)

    @pl.when(gy == 0)
    def _():
        edge_in[0] = jnp.zeros(edge_in.shape[1:], jnp.float32)

    @pl.when(gy == n_gy - 1)
    def _():
        edge_in[1] = jnp.zeros(edge_in.shape[1:], jnp.float32)

    for i in range(3):
        load_maps[i].wait()
        for x in range(3):
            coef[i, x] = jnp.broadcast_to(maps[i, x : x + 1, :], (8, width))

    has_low = (gx > 0, gy > 0)
    has_high = (gx < n_gx - 1, gy < n_gy - 1)

    def x_copy(side, s, k):
        rows = pl.ds(pl.multiple_of(k * CH, 8), CH)
        padded = pl.ds(pl.multiple_of(k * CH + PAD, 8), CH)
        peer = gx + 1 if side == 0 else gx - 1
        return pltpu.make_async_remote_copy(
            src_ref=q.at[s, :, 2 if side == 0 else 0, padded, :],
            dst_ref=halo.at[side, s, :, rows, :],
            send_sem=x_send.at[side, s, k],
            recv_sem=x_recv.at[side, s, k],
            device_id={"gx": peer},
            device_id_type=MESH,
        )

    def y_copy(side, s, k):
        rows = pl.ds(pl.multiple_of(k * CH, 8), CH)
        peer = gy + 1 if side == 0 else gy - 1
        return pltpu.make_async_remote_copy(
            src_ref=edge_out.at[side, s, rows, :],
            dst_ref=edge_in.at[side, s, rows, :],
            send_sem=y_send.at[side, s, k],
            recv_sem=y_recv.at[side, s, k],
            device_id={"gy": peer},
            device_id_type=MESH,
        )

    relays = n_gx == 8

    def hop_copy(side, s, k):
        rows = pl.ds(pl.multiple_of(k * CH, 8), CH)
        padded = pl.ds(pl.multiple_of(k * CH + PAD, 8), CH)
        return pltpu.make_async_remote_copy(
            src_ref=q.at[s, :, 2 if side == 0 else 0, padded, :],
            dst_ref=passing.at[s, :, rows, :],
            send_sem=x_send.at[side, s, k],
            recv_sem=pass_recv.at[s, k],
            device_id={"gx": gx + far if side == 0 else gx - far},
            device_id_type=MESH,
        )

    def pass_copy(side, s, k):
        rows = pl.ds(pl.multiple_of(k * CH, 8), CH)
        return pltpu.make_async_remote_copy(
            src_ref=passing.at[s, :, rows, :],
            dst_ref=halo.at[side, s, :, rows, :],
            send_sem=pass_send.at[s, k],
            recv_sem=x_recv.at[side, s, k],
            device_id={"gx": far if side == 0 else far - 1},
            device_id_type=MESH,
        )

    def forward(s, k):
        if not relays:
            return

        @pl.when(gx == n_gx - 1)
        def _():
            hop_copy(0, s, k).wait_recv()
            pass_copy(0, s, k).start()

        @pl.when(gx == 0)
        def _():
            hop_copy(1, s, k).wait_recv()
            pass_copy(1, s, k).start()

    def send(copy, s, k, axis):
        direct_high, direct_low = has_high[axis], has_low[axis]
        if axis == 0 and relays:
            odd = lax.rem(k, 2) == 1
            hop_high, hop_low = odd & (gx == far - 1), odd & (gx == far)
            direct_high &= jnp.logical_not(hop_high)
            direct_low &= jnp.logical_not(hop_low)

            @pl.when(hop_high)
            def _():
                hop_copy(0, s, k).start()

            @pl.when(hop_low)
            def _():
                hop_copy(1, s, k).start()

        @pl.when(direct_high)
        def _():
            copy(0, s, k).start()

        @pl.when(direct_low)
        def _():
            copy(1, s, k).start()

    def received(copy, s, k, axis):
        @pl.when(has_low[axis])
        def _():
            copy(0, s, k).wait_recv()

        @pl.when(has_high[axis])
        def _():
            copy(1, s, k).wait_recv()

    def sent(copy, s, k, axis):
        @pl.when(has_high[axis])
        def _():
            copy(0, s, k).wait_send()

        @pl.when(has_low[axis])
        def _():
            copy(1, s, k).wait_send()

    lane = lax.broadcasted_iota(jnp.int32, (CH, tile), 1)

    def pack(s, k):
        rows = pl.ds(pl.multiple_of(k * CH + PAD, 8), CH)
        high = jnp.zeros((CH, tile), jnp.float32)
        low = jnp.zeros((CH, tile), jnp.float32)
        for f in range(fields):
            for x in range(3):
                j = f * 3 + x
                last = q[s, f, x, rows, width - tile : width]
                first = q[s, f, x, rows, 0:tile]
                high = jnp.where(lane == j, pltpu.roll(last, j + 1, 1), high)
                low = jnp.where(lane == j, pltpu.roll(first, j, 1) if j else first, low)
        flat = pl.ds(pl.multiple_of(k * CH, 8), CH)
        edge_out[0, s, flat, :] = high
        edge_out[1, s, flat, :] = low

    pl.semaphore_wait(barrier, n_gx - 1 + n_gy - 1)
    load_strip.wait()

    owner = owner_ref[gy]
    n_rows = bound.shape[0]
    core = lax.rem(gx, 2)
    part = lax.rem(gx // far, 2)
    middle = []
    while 2 << len(middle) < far:
        middle.append(2 << len(middle))
    n_phases = 4 + len(middle)

    def flip(bit):
        digit = lax.rem(gx // bit, 2)
        return gx + bit - 2 * bit * digit

    def differs(bit):
        return lax.rem(gx // bit, 2) != lax.rem(owner // bit, 2)

    def at(start, size):
        return pl.ds(pl.multiple_of(start, 8), size)

    def b_copy(phase, p):
        first, count, row = pieces[p]
        size, base = count * 8, first * 8
        one, two = at(base, size), at(2 * base, 2 * size)
        if phase == 0:
            src, dst, bit = strip.at[at(row + (1 - core) * 2 * size, 2 * size), :], got_half.at[two, :], 1
        elif phase == 1:
            src, dst, bit = half.at[at(2 * base + (1 - part) * size, size), :], got_quarter.at[one, :], far
        elif phase < n_phases - 2:
            i = phase - 2
            src, dst, bit = quarter.at[i, one, :], got_other.at[i, one, :], middle[i]
        elif phase == n_phases - 2:
            mine = at(2 * base + part * size, size)
            src, dst, bit = quarter.at[len(middle), one, :], whole_half.at[mine, :], far
        else:
            src, dst, bit = whole_half.at[two, :], got_rest.at[two, :], 1
        return pltpu.make_async_remote_copy(
            src_ref=src, dst_ref=dst, send_sem=b_send.at[phase, p], recv_sem=b_recv.at[phase, p],
            device_id={"gx": flip(bit)}, device_id_type=MESH,
        )

    def b_finish(phase, p):
        first, count, row = pieces[p]
        size, base = count * 8, first * 8
        one, two = at(base, size), at(2 * base, 2 * size)
        b_copy(phase, p).wait_recv()
        if phase == 0:
            half[two, :] = jnp.where(differs(1), got_half[two, :], strip[at(row + core * 2 * size, 2 * size), :])
        elif phase == 1:
            quarter[0, one, :] = jnp.where(
                differs(far), got_quarter[one, :], half[at(2 * base + part * size, size), :]
            )
        elif phase < n_phases - 2:
            i = phase - 2
            quarter[i + 1, one, :] = jnp.where(differs(middle[i]), got_other[i, one, :], quarter[i, one, :])
        if phase == n_phases - 3:
            whole_half[at(2 * base + part * size, size), :] = quarter[len(middle), one, :]
        if phase < n_phases - 1:
            b_copy(phase + 1, p).start()
        if phase == n_phases - 2:
            bound[at(row + core * 2 * size, 2 * size), :] = whole_half[two, :]
        elif phase == n_phases - 1:
            bound[at(row + (1 - core) * 2 * size, 2 * size), :] = got_rest[two, :]

    def first_sends(k, _):
        send(x_copy, 0, k, 0)
        return 0

    def first_edges(k, _):
        pack(0, k)
        send(y_copy, 0, k, 1)
        return 0

    for p in range(len(pieces)):
        b_copy(0, p).start()
    load.wait()
    lax.fori_loop(0, chunks, first_sends, 0)
    for t in range(n_phases + len(pieces) - 1):
        for phase in reversed(range(n_phases)):
            if 0 <= t - phase < len(pieces):
                b_finish(phase, t - phase)
        if t == 0:
            lax.fori_loop(0, chunks, first_edges, 0)
        if t in (2, 4):
            forward(0, t - 1)

    wide_lane = lax.broadcasted_iota(jnp.int32, (8, width), 1)
    level = lax.broadcasted_iota(jnp.int32, (8, width), 0)
    is_bottom, is_top = level == 0, level == 7
    is_first, is_last = wide_lane == 0, wide_lane == width - 1

    def block(s, z0, x, weight):
        slope, metric, relax = coef[0, x], coef[1, x], coef[2, x]
        rows = pl.ds(pl.multiple_of(z0 + PAD, 8), 8)
        flat = pl.ds(pl.multiple_of(z0, 8), 8)
        from_south, from_north = edge_in[0, s, flat, :], edge_in[1, s, flat, :]
        centers, axs, ays, azs, commons = [], [], [], [], []
        for f in range(fields):
            c = q[s, f, x, rows, :]
            above = q[s, f, x, pl.ds(pl.multiple_of(z0 + PAD + 8, 8), 8), :]
            below = q[s, f, x, pl.ds(pl.multiple_of(z0 + PAD - 8, 8), 8), :]
            up = pltpu.roll(jnp.where(is_bottom, above, c), 7, 0)
            down = pltpu.roll(jnp.where(is_top, below, c), 1, 0)
            east = q[s, f, x + 1, rows, :] if x < 2 else halo[1, s, f, flat, :]
            west = q[s, f, x - 1, rows, :] if x > 0 else halo[0, s, f, flat, :]
            j = f * 3 + x
            a = pltpu.roll(from_south, tile - j, 1) if j else from_south
            b = pltpu.roll(from_north, tile - 1 - j, 1)
            south = jnp.where(is_first, jnp.concatenate([a] * 3, axis=1), pltpu.roll(c, 1, 1))
            north = jnp.where(is_last, jnp.concatenate([b] * 3, axis=1), pltpu.roll(c, width - 1, 1))
            az = (0.5 * (up - down)) * metric
            ax = 0.5 * (east - west) - slope * az
            ay = 0.5 * (north - south)
            spread = (east + west) + (north + south) - 4.0 * c
            limit = bound[pl.ds(pl.multiple_of(f * levels + z0, 8), 8), :]
            common = relax * (limit - c) + viscosity * spread - (wind_east * ax + wind_north * ay)
            centers.append(c)
            axs.append(ax)
            ays.append(ay)
            azs.append(az)
            commons.append(common)
        tend = [
            commons[0] - axs[4],
            commons[1] - ays[4],
            commons[2] - azs[4] + buoyancy * centers[3],
            commons[3] - buoyancy * centers[2],
            commons[4] - (axs[0] + ays[1] + azs[2]),
        ]
        for f in range(fields):
            q[s + 1, f, x, rows, :] = q[0, f, x, rows, :] + weight * tend[f]

    def out_copy(k):
        rows = pl.ds(pl.multiple_of(k * CH, 8), CH)
        padded = pl.ds(pl.multiple_of(k * CH + PAD, 8), CH)
        return pltpu.make_async_copy(q.at[3, :, :, padded, :], out_ref.at[:, :, rows, :], out_sem.at[k])

    def substep(s, _):
        weight = time_step * jnp.where(s == 0, 1.0 / 3.0, jnp.where(s == 1, 0.5, 1.0)).astype(jnp.float32)

        def chunk(k, _):
            received(y_copy, s, k, 1)
            received(x_copy, s, k, 0)

            def rows8(i, _):
                for x in (0, 2, 1):
                    block(s, k * CH + i * 8, x, weight)
                return 0

            lax.fori_loop(0, CH // 8, rows8, 0)

            @pl.when(s < 2)
            def _():
                send(x_copy, s + 1, k, 0)
                pack(s + 1, k)
                send(y_copy, s + 1, k, 1)
                if relays:

                    @pl.when((k > 1) & (lax.rem(k, 2) == 0))
                    def _():
                        forward(s + 1, k - 1)

            @pl.when(s == 2)
            def _():
                out_copy(k).start()

            return 0

        lax.fori_loop(0, chunks, chunk, 0)
        return 0

    lax.fori_loop(0, 3, substep, 0)

    feat = 4 * levels
    total[feat:, :] = jnp.zeros((total.shape[0] - feat, width), jnp.float32)
    for i, f in enumerate((0, 1, 3, 4)):
        total[i * levels : (i + 1) * levels, :] = q[3, f, 0, inner, :] + q[3, f, 1, inner, :] + q[3, f, 2, inner, :]
    sub = lax.broadcasted_iota(jnp.int32, (8, width), 0)
    picks, targets = [], []
    for d in range(n_gy):
        pick = jnp.zeros((8, width), jnp.float32)
        target = jnp.full((8, width), -1, jnp.int32)
        for slot in range(cap):
            live = jnp.where(count_ref[0, 0, d] > slot, slot, -1)
            shifted = wide_lane - 3 * cell_ref[0, 0, d, slot]
            here = sub == live
            pick = jnp.where(here & (shifted >= 0) & (shifted < 3), 1.0, pick)
            target = jnp.where(here, row_ref[0, 0, d, slot], target)
        picks.append(pick)
        targets.append(target.astype(jnp.float32))
    pick = jnp.concatenate(picks, axis=0)
    target = jnp.concatenate(targets, axis=0)
    sums = lax.dot_general(
        pick, total[...], (((1,), (1,)), ((), ())), precision=HIGH, preferred_element_type=jnp.float32
    )
    column = lax.broadcasted_iota(jnp.int32, sums.shape, 1)
    records[...] = jnp.where(column == feat, target[:, :1], sums * (1.0 / 9.0))

    def r_copy(off):
        peer = lax.rem(gy + off, n_gy)
        return pltpu.make_async_remote_copy(
            src_ref=records.at[pl.ds(pl.multiple_of(peer * 8, 8), 8), :],
            dst_ref=got_records.at[pl.ds(pl.multiple_of(gy * 8, 8), 8), :],
            send_sem=r_send.at[off - 1],
            recv_sem=r_recv.at[off - 1],
            device_id={"gy": peer},
            device_id_type=MESH,
        )

    for off in range(1, n_gy):
        r_copy(off).start()
    mine = pl.ds(pl.multiple_of(gy * 8, 8), 8)
    got_records[mine, :] = records[mine, :]
    for p in range(len(pieces)):
        for phase in range(n_phases):
            b_copy(phase, p).wait_send()

    def settle(s, _):
        def inner_settle(k, _):
            sent(x_copy, s, k, 0)
            sent(y_copy, s, k, 1)
            if relays:

                @pl.when((lax.rem(k, 2) == 1) & ((gx == 0) | (gx == n_gx - 1)))
                def _():
                    pass_copy(0, s, k).wait_send()
            return 0

        lax.fori_loop(0, chunks, inner_settle, 0)
        return 0

    lax.fori_loop(0, 3, settle, 0)
    for off in range(1, n_gy):
        r_copy(off).wait()
    got = got_records[...]
    parents = lax.broadcasted_iota(jnp.int32, (got.shape[0], parent_ref.shape[1]), 1).astype(jnp.float32)
    onehot = jnp.where(got[:, feat : feat + 1] == parents, 1.0, 0.0)
    totals = lax.dot_general(
        got, onehot, (((0,), (0,)), ((), ())), precision=HIGH, preferred_element_type=jnp.float32
    )
    load_parent.wait()
    tally = jnp.sum(onehot, axis=0, keepdims=True)
    pout_ref[...] = jnp.where(tally > 0, totals[:feat] / jnp.maximum(tally, 1.0), parent_ref[...])

    def settle_out(k, _):
        out_copy(k).wait()
        return 0

    lax.fori_loop(0, chunks, settle_out, 0)


def on_device(
    n_gx, n_gy,
    nest_fields, boundary_strip, strip_owner, terrain_slope, column_metric, relax_rate,
    parent_state, intersection_cell, intersection_row, intersection_count,
):
    fields, levels, cells_x, width = nest_fields.shape
    cap = intersection_cell.shape[3]
    chunks = levels // CH
    n_rows = fields * levels
    quarters = -(-n_rows // 32)
    pieces = []
    for p in range(PIECES):
        first = quarters * p // PIECES
        count = quarters * (p + 1) // PIECES - first
        pieces.append((first, count, min(first * 32, n_rows - count * 32)))
    n_quarter = quarters * 8
    n_half = 2 * n_quarter
    bits = max(n_gx.bit_length() - 3, 1)
    feat = 4 * levels
    feat_pad = -(-(feat + 1) // 128) * 128
    tile = width // 3
    f32 = jnp.float32
    smem = pl.BlockSpec(memory_space=pltpu.SMEM)
    vmem = pl.BlockSpec(memory_space=pltpu.VMEM)
    hbm = pl.BlockSpec(memory_space=pl.ANY)
    dma = pltpu.SemaphoreType.DMA
    out, parent = pl.pallas_call(
        functools.partial(kernel, n_gx, n_gy, cap, tuple(pieces)),
        out_shape=(
            jax.ShapeDtypeStruct((fields, cells_x, levels, width), f32),
            jax.ShapeDtypeStruct((feat, parent_state.shape[1]), f32),
        ),
        in_specs=[smem] * 4 + [hbm] * 6,
        out_specs=(hbm, vmem),
        scratch_shapes=[
            pltpu.VMEM((4, fields, 3, levels + 2 * PAD, width), f32),
            pltpu.VMEM((2, 3, fields, levels, width), f32),
            pltpu.VMEM((2, 3, levels, tile), f32),
            pltpu.VMEM((2, 3, levels, tile), f32),
            pltpu.VMEM((3, 3, 8, width), f32),
            pltpu.VMEM((n_rows, width), f32),
            pltpu.VMEM((n_half, width), f32),
            pltpu.VMEM((n_half, width), f32),
            pltpu.VMEM((n_quarter, width), f32),
            pltpu.VMEM((bits + 1, n_quarter, width), f32),
            pltpu.VMEM((bits, n_quarter, width), f32),
            pltpu.VMEM((n_half, width), f32),
            pltpu.VMEM((n_half, width), f32),
            pltpu.VMEM((n_rows, width), f32),
            pltpu.VMEM((feat_pad, width), f32),
            pltpu.VMEM((n_gy * 8, feat_pad), f32),
            pltpu.VMEM((n_gy * 8, feat_pad), f32),
            pltpu.VMEM((3, 3, width), f32),
            pltpu.VMEM((feat, parent_state.shape[1]), f32),
            dma,
            dma,
            dma((2, 3, chunks)),
            dma((2, 3, chunks)),
            dma((2, 3, chunks)),
            dma((2, 3, chunks)),
            dma((bits + 4, PIECES)),
            dma((bits + 4, PIECES)),
            dma((n_gy,)),
            dma((n_gy,)),
            dma((chunks,)),
            dma((4,)),
            pltpu.VMEM((3, fields, levels, width), f32),
            dma((3, chunks)),
            dma((3, chunks)),
        ],
        compiler_params=pltpu.CompilerParams(
            collective_id=0, has_side_effects=True, vmem_limit_bytes=62 * 1024 * 1024
        ),
    )(
        strip_owner,
        intersection_cell,
        intersection_row,
        intersection_count,
        nest_fields.transpose(0, 2, 1, 3),
        boundary_strip.reshape(n_rows, width),
        terrain_slope,
        column_metric,
        relax_rate,
        parent_state[0].T,
    )
    return out.transpose(0, 2, 1, 3), parent.T[None]


def solution(mesh):
    placed = (
        P(None, None, "gx", "gy"),
        P("gx", None, None, "gy"),
        P(),
        P("gx", "gy"),
        P("gx", "gy"),
        P("gx", "gy"),
        P("gx", "gy", None),
        P("gx", "gy", None, None),
        P("gx", "gy", None, None),
        P("gx", "gy", None),
    )
    return jax.shard_map(
        functools.partial(on_device, mesh.shape["gx"], mesh.shape["gy"]),
        mesh=mesh,
        in_specs=placed,
        out_specs=(P(None, None, "gx", "gy"), P("gx", "gy", None)),
        check_vma=False,
    )
```

```python
import functools
import jax
import jax.numpy as jnp
from jax import lax
from jax.experimental import pallas as pl
from jax.experimental.pallas import tpu as pltpu
from jax.sharding import PartitionSpec as P

MESH = pl.DeviceIdType.MESH
time_step = 0.25
viscosity = 0.05
buoyancy = 0.5
wind_east = 0.6
wind_north = -0.4
PAD = 8
CH = 16
PIECES = 2
HIGH = lax.Precision.HIGHEST


def kernel(
    n_gx, n_gy, cap, pieces,
    owner_ref, cell_ref, row_ref, count_ref,
    nest_ref, strip_ref, slope_hbm, metric_hbm, relax_hbm, parent_hbm,
    out_ref, pout_ref,
    q, halo, edge_out, edge_in, coef,
    strip, got_half, half, got_quarter, quarter, got_other, whole_half, got_rest, bound,
    total, records, got_records, maps, parent_ref,
    load_sem, strip_sem, x_send, x_recv, y_send, y_recv, b_send, b_recv, r_send, r_recv, out_sem, small_sem,
    passing, pass_send, pass_recv,
):
    fields, levels, width = q.shape[1], q.shape[3] - 2 * PAD, q.shape[4]
    chunks = levels // CH
    gx, gy = lax.axis_index("gx"), lax.axis_index("gy")
    tile = width // 3
    inner = pl.ds(PAD, levels)
    far = n_gx // 2

    load = pltpu.make_async_copy(nest_ref, q.at[0, :, :, inner, :], load_sem)
    load.start()
    load_strip = pltpu.make_async_copy(strip_ref, strip, strip_sem)
    load_strip.start()
    load_maps = [
        pltpu.make_async_copy(ref, maps.at[i], small_sem.at[i])
        for i, ref in enumerate((slope_hbm, metric_hbm, relax_hbm))
    ]
    for copy in load_maps:
        copy.start()
    load_parent = pltpu.make_async_copy(parent_hbm, parent_ref, small_sem.at[3])
    load_parent.start()

    barrier = pltpu.get_barrier_semaphore()
    for off in range(1, n_gx):
        pl.semaphore_signal(barrier, inc=1, device_id={"gx": lax.rem(gx + off, n_gx)}, device_id_type=MESH)
    for off in range(1, n_gy):
        pl.semaphore_signal(barrier, inc=1, device_id={"gy": lax.rem(gy + off, n_gy)}, device_id_type=MESH)

    zero = jnp.zeros((PAD, width), jnp.float32)

    def clear(s, _):
        for f in range(fields):
            for x in range(3):
                q[s, f, x, 0:PAD, :] = zero
                q[s, f, x, PAD + levels :, :] = zero
        return 0

    lax.fori_loop(0, 3, clear, 0)

    def clear_side(side):
        def body(i, _):
            for f in range(fields):
                halo[side, i // (levels // 8), f, pl.ds(pl.multiple_of(i % (levels // 8) * 8, 8), 8), :] = zero
            return 0

        lax.fori_loop(0, 3 * levels // 8, body, 0)

    @pl.when(gx == 0)
    def _():
        clear_side(0)

    @pl.when(gx == n_gx - 1)
    def _():
        clear_side(1)

    @pl.when(gy == 0)
    def _():
        edge_in[0] = jnp.zeros(edge_in.shape[1:], jnp.float32)

    @pl.when(gy == n_gy - 1)
    def _():
        edge_in[1] = jnp.zeros(edge_in.shape[1:], jnp.float32)

    for i in range(3):
        load_maps[i].wait()
        for x in range(3):
            coef[i, x] = jnp.broadcast_to(maps[i, x : x + 1, :], (8, width))

    has_low = (gx > 0, gy > 0)
    has_high = (gx < n_gx - 1, gy < n_gy - 1)

    def x_copy(side, s, k):
        rows = pl.ds(pl.multiple_of(k * CH, 8), CH)
        padded = pl.ds(pl.multiple_of(k * CH + PAD, 8), CH)
        peer = gx + 1 if side == 0 else gx - 1
        return pltpu.make_async_remote_copy(
            src_ref=q.at[s, :, 2 if side == 0 else 0, padded, :],
            dst_ref=halo.at[side, s, :, rows, :],
            send_sem=x_send.at[side, s, k],
            recv_sem=x_recv.at[side, s, k],
            device_id={"gx": peer},
            device_id_type=MESH,
        )

    def y_copy(side, s, k):
        rows = pl.ds(pl.multiple_of(k * CH, 8), CH)
        peer = gy + 1 if side == 0 else gy - 1
        return pltpu.make_async_remote_copy(
            src_ref=edge_out.at[side, s, rows, :],
            dst_ref=edge_in.at[side, s, rows, :],
            send_sem=y_send.at[side, s, k],
            recv_sem=y_recv.at[side, s, k],
            device_id={"gy": peer},
            device_id_type=MESH,
        )

    relays = n_gx == 8

    def hop_copy(side, s, k):
        rows = pl.ds(pl.multiple_of(k * CH, 8), CH)
        padded = pl.ds(pl.multiple_of(k * CH + PAD, 8), CH)
        return pltpu.make_async_remote_copy(
            src_ref=q.at[s, :, 2 if side == 0 else 0, padded, :],
            dst_ref=passing.at[s, :, rows, :],
            send_sem=x_send.at[side, s, k],
            recv_sem=pass_recv.at[s, k],
            device_id={"gx": gx + far if side == 0 else gx - far},
            device_id_type=MESH,
        )

    def pass_copy(side, s, k):
        rows = pl.ds(pl.multiple_of(k * CH, 8), CH)
        return pltpu.make_async_remote_copy(
            src_ref=passing.at[s, :, rows, :],
            dst_ref=halo.at[side, s, :, rows, :],
            send_sem=pass_send.at[s, k],
            recv_sem=x_recv.at[side, s, k],
            device_id={"gx": far if side == 0 else far - 1},
            device_id_type=MESH,
        )

    def forward(s, k):
        if not relays:
            return

        @pl.when(gx == n_gx - 1)
        def _():
            hop_copy(0, s, k).wait_recv()
            pass_copy(0, s, k).start()

        @pl.when(gx == 0)
        def _():
            hop_copy(1, s, k).wait_recv()
            pass_copy(1, s, k).start()

    def send(copy, s, k, axis):
        direct_high, direct_low = has_high[axis], has_low[axis]
        if axis == 0 and relays:
            odd = lax.rem(k, 2) == 1
            hop_high, hop_low = odd & (gx == far - 1), odd & (gx == far)
            direct_high &= jnp.logical_not(hop_high)
            direct_low &= jnp.logical_not(hop_low)

            @pl.when(hop_high)
            def _():
                hop_copy(0, s, k).start()

            @pl.when(hop_low)
            def _():
                hop_copy(1, s, k).start()

        @pl.when(direct_high)
        def _():
            copy(0, s, k).start()

        @pl.when(direct_low)
        def _():
            copy(1, s, k).start()

    def received(copy, s, k, axis):
        @pl.when(has_low[axis])
        def _():
            copy(0, s, k).wait_recv()

        @pl.when(has_high[axis])
        def _():
            copy(1, s, k).wait_recv()

    def sent(copy, s, k, axis):
        @pl.when(has_high[axis])
        def _():
            copy(0, s, k).wait_send()

        @pl.when(has_low[axis])
        def _():
            copy(1, s, k).wait_send()

    lane = lax.broadcasted_iota(jnp.int32, (CH, tile), 1)

    def pack(s, k):
        rows = pl.ds(pl.multiple_of(k * CH + PAD, 8), CH)
        high = jnp.zeros((CH, tile), jnp.float32)
        low = jnp.zeros((CH, tile), jnp.float32)
        for f in range(fields):
            for x in range(3):
                j = f * 3 + x
                last = q[s, f, x, rows, width - tile : width]
                first = q[s, f, x, rows, 0:tile]
                high = jnp.where(lane == j, pltpu.roll(last, j + 1, 1), high)
                low = jnp.where(lane == j, pltpu.roll(first, j, 1) if j else first, low)
        flat = pl.ds(pl.multiple_of(k * CH, 8), CH)
        edge_out[0, s, flat, :] = high
        edge_out[1, s, flat, :] = low

    pl.semaphore_wait(barrier, n_gx - 1 + n_gy - 1)
    load_strip.wait()

    owner = owner_ref[gy]
    n_rows = bound.shape[0]
    core = lax.rem(gx, 2)
    part = lax.rem(gx // far, 2)
    middle = []
    while 2 << len(middle) < far:
        middle.append(2 << len(middle))
    n_phases = 4 + len(middle)

    def flip(bit):
        digit = lax.rem(gx // bit, 2)
        return gx + bit - 2 * bit * digit

    def differs(bit):
        return lax.rem(gx // bit, 2) != lax.rem(owner // bit, 2)

    def at(start, size):
        return pl.ds(pl.multiple_of(start, 8), size)

    def b_copy(phase, p):
        first, count, row = pieces[p]
        size, base = count * 8, first * 8
        one, two = at(base, size), at(2 * base, 2 * size)
        if phase == 0:
            src, dst, bit = strip.at[at(row + (1 - core) * 2 * size, 2 * size), :], got_half.at[two, :], 1
        elif phase == 1:
            src, dst, bit = half.at[at(2 * base + (1 - part) * size, size), :], got_quarter.at[one, :], far
        elif phase < n_phases - 2:
            i = phase - 2
            src, dst, bit = quarter.at[i, one, :], got_other.at[i, one, :], middle[i]
        elif phase == n_phases - 2:
            mine = at(2 * base + part * size, size)
            src, dst, bit = quarter.at[len(middle), one, :], whole_half.at[mine, :], far
        else:
            src, dst, bit = whole_half.at[two, :], got_rest.at[two, :], 1
        return pltpu.make_async_remote_copy(
            src_ref=src, dst_ref=dst, send_sem=b_send.at[phase, p], recv_sem=b_recv.at[phase, p],
            device_id={"gx": flip(bit)}, device_id_type=MESH,
        )

    def b_finish(phase, p):
        first, count, row = pieces[p]
        size, base = count * 8, first * 8
        one, two = at(base, size), at(2 * base, 2 * size)
        b_copy(phase, p).wait_recv()
        if phase == 0:
            half[two, :] = jnp.where(differs(1), got_half[two, :], strip[at(row + core * 2 * size, 2 * size), :])
        elif phase == 1:
            quarter[0, one, :] = jnp.where(
                differs(far), got_quarter[one, :], half[at(2 * base + part * size, size), :]
            )
        elif phase < n_phases - 2:
            i = phase - 2
            quarter[i + 1, one, :] = jnp.where(differs(middle[i]), got_other[i, one, :], quarter[i, one, :])
        if phase == n_phases - 3:
            whole_half[at(2 * base + part * size, size), :] = quarter[len(middle), one, :]
        if phase < n_phases - 1:
            b_copy(phase + 1, p).start()
        if phase == n_phases - 2:
            bound[at(row + core * 2 * size, 2 * size), :] = whole_half[two, :]
        elif phase == n_phases - 1:
            bound[at(row + (1 - core) * 2 * size, 2 * size), :] = got_rest[two, :]

    def first_sends(k, _):
        send(x_copy, 0, k, 0)
        return 0

    def first_edges(k, _):
        pack(0, k)
        send(y_copy, 0, k, 1)
        return 0

    for p in range(len(pieces)):
        b_copy(0, p).start()
    load.wait()
    send(x_copy, 0, 0, 0)
    send(x_copy, 0, 1, 0)
    for t in range(n_phases + len(pieces) - 1):
        for phase in reversed(range(n_phases)):
            if 0 <= t - phase < len(pieces):
                b_finish(phase, t - phase)
        if 0 < t < chunks - 1:
            send(x_copy, 0, t + 1, 0)
        if t == 0:
            lax.fori_loop(0, chunks, first_edges, 0)
        if t in (2, 4):
            forward(0, t - 1)

    wide_lane = lax.broadcasted_iota(jnp.int32, (8, width), 1)
    level = lax.broadcasted_iota(jnp.int32, (8, width), 0)
    is_bottom, is_top = level == 0, level == 7
    is_first, is_last = wide_lane == 0, wide_lane == width - 1

    def block(s, z0, x, weight):
        slope, metric, relax = coef[0, x], coef[1, x], coef[2, x]
        rows = pl.ds(pl.multiple_of(z0 + PAD, 8), 8)
        flat = pl.ds(pl.multiple_of(z0, 8), 8)
        from_south, from_north = edge_in[0, s, flat, :], edge_in[1, s, flat, :]
        centers, axs, ays, azs, commons = [], [], [], [], []
        for f in range(fields):
            c = q[s, f, x, rows, :]
            above = q[s, f, x, pl.ds(pl.multiple_of(z0 + PAD + 8, 8), 8), :]
            below = q[s, f, x, pl.ds(pl.multiple_of(z0 + PAD - 8, 8), 8), :]
            up = pltpu.roll(jnp.where(is_bottom, above, c), 7, 0)
            down = pltpu.roll(jnp.where(is_top, below, c), 1, 0)
            east = q[s, f, x + 1, rows, :] if x < 2 else halo[1, s, f, flat, :]
            west = q[s, f, x - 1, rows, :] if x > 0 else halo[0, s, f, flat, :]
            j = f * 3 + x
            a = pltpu.roll(from_south, tile - j, 1) if j else from_south
            b = pltpu.roll(from_north, tile - 1 - j, 1)
            south = jnp.where(is_first, jnp.concatenate([a] * 3, axis=1), pltpu.roll(c, 1, 1))
            north = jnp.where(is_last, jnp.concatenate([b] * 3, axis=1), pltpu.roll(c, width - 1, 1))
            az = (0.5 * (up - down)) * metric
            ax = 0.5 * (east - west) - slope * az
            ay = 0.5 * (north - south)
            spread = (east + west) + (north + south) - 4.0 * c
            limit = bound[pl.ds(pl.multiple_of(f * levels + z0, 8), 8), :]
            common = relax * (limit - c) + viscosity * spread - (wind_east * ax + wind_north * ay)
            centers.append(c)
            axs.append(ax)
            ays.append(ay)
            azs.append(az)
            commons.append(common)
        tend = [
            commons[0] - axs[4],
            commons[1] - ays[4],
            commons[2] - azs[4] + buoyancy * centers[3],
            commons[3] - buoyancy * centers[2],
            commons[4] - (axs[0] + ays[1] + azs[2]),
        ]
        for f in range(fields):
            q[s + 1, f, x, rows, :] = q[0, f, x, rows, :] + weight * tend[f]

    def out_copy(k):
        rows = pl.ds(pl.multiple_of(k * CH, 8), CH)
        padded = pl.ds(pl.multiple_of(k * CH + PAD, 8), CH)
        return pltpu.make_async_copy(q.at[3, :, :, padded, :], out_ref.at[:, :, rows, :], out_sem.at[k])

    def substep(s, _):
        weight = time_step * jnp.where(s == 0, 1.0 / 3.0, jnp.where(s == 1, 0.5, 1.0)).astype(jnp.float32)

        def chunk(k, _):
            def middle_rows(i, _):
                block(s, k * CH + i * 8, 1, weight)
                return 0

            def outer_rows(i, _):
                for x in (0, 2):
                    block(s, k * CH + i * 8, x, weight)
                return 0

            received(y_copy, s, k, 1)
            lax.fori_loop(0, CH // 8, middle_rows, 0)
            received(x_copy, s, k, 0)
            lax.fori_loop(0, CH // 8, outer_rows, 0)

            @pl.when(s < 2)
            def _():
                send(x_copy, s + 1, k, 0)
                pack(s + 1, k)
                send(y_copy, s + 1, k, 1)
                if relays:

                    @pl.when((k > 1) & (lax.rem(k, 2) == 0))
                    def _():
                        forward(s + 1, k - 1)

            @pl.when(s == 2)
            def _():
                out_copy(k).start()

            return 0

        lax.fori_loop(0, chunks, chunk, 0)
        return 0

    lax.fori_loop(0, 3, substep, 0)

    feat = 4 * levels
    total[feat:, :] = jnp.zeros((total.shape[0] - feat, width), jnp.float32)
    for i, f in enumerate((0, 1, 3, 4)):
        total[i * levels : (i + 1) * levels, :] = q[3, f, 0, inner, :] + q[3, f, 1, inner, :] + q[3, f, 2, inner, :]
    sub = lax.broadcasted_iota(jnp.int32, (8, width), 0)
    picks, targets = [], []
    for d in range(n_gy):
        pick = jnp.zeros((8, width), jnp.float32)
        target = jnp.full((8, width), -1, jnp.int32)
        for slot in range(cap):
            live = jnp.where(count_ref[0, 0, d] > slot, slot, -1)
            shifted = wide_lane - 3 * cell_ref[0, 0, d, slot]
            here = sub == live
            pick = jnp.where(here & (shifted >= 0) & (shifted < 3), 1.0, pick)
            target = jnp.where(here, row_ref[0, 0, d, slot], target)
        picks.append(pick)
        targets.append(target.astype(jnp.float32))
    pick = jnp.concatenate(picks, axis=0)
    target = jnp.concatenate(targets, axis=0)
    sums = lax.dot_general(
        pick, total[...], (((1,), (1,)), ((), ())), precision=HIGH, preferred_element_type=jnp.float32
    )
    column = lax.broadcasted_iota(jnp.int32, sums.shape, 1)
    records[...] = jnp.where(column == feat, target[:, :1], sums * (1.0 / 9.0))

    def r_copy(off):
        peer = lax.rem(gy + off, n_gy)
        return pltpu.make_async_remote_copy(
            src_ref=records.at[pl.ds(pl.multiple_of(peer * 8, 8), 8), :],
            dst_ref=got_records.at[pl.ds(pl.multiple_of(gy * 8, 8), 8), :],
            send_sem=r_send.at[off - 1],
            recv_sem=r_recv.at[off - 1],
            device_id={"gy": peer},
            device_id_type=MESH,
        )

    for off in range(1, n_gy):
        r_copy(off).start()
    mine = pl.ds(pl.multiple_of(gy * 8, 8), 8)
    got_records[mine, :] = records[mine, :]
    for p in range(len(pieces)):
        for phase in range(n_phases):
            b_copy(phase, p).wait_send()

    def settle(s, _):
        def inner_settle(k, _):
            sent(x_copy, s, k, 0)
            sent(y_copy, s, k, 1)
            if relays:

                @pl.when((lax.rem(k, 2) == 1) & ((gx == 0) | (gx == n_gx - 1)))
                def _():
                    pass_copy(0, s, k).wait_send()
            return 0

        lax.fori_loop(0, chunks, inner_settle, 0)
        return 0

    lax.fori_loop(0, 3, settle, 0)
    for off in range(1, n_gy):
        r_copy(off).wait()
    got = got_records[...]
    parents = lax.broadcasted_iota(jnp.int32, (got.shape[0], parent_ref.shape[1]), 1).astype(jnp.float32)
    onehot = jnp.where(got[:, feat : feat + 1] == parents, 1.0, 0.0)
    totals = lax.dot_general(
        got, onehot, (((0,), (0,)), ((), ())), precision=HIGH, preferred_element_type=jnp.float32
    )
    load_parent.wait()
    tally = jnp.sum(onehot, axis=0, keepdims=True)
    pout_ref[...] = jnp.where(tally > 0, totals[:feat] / jnp.maximum(tally, 1.0), parent_ref[...])

    def settle_out(k, _):
        out_copy(k).wait()
        return 0

    lax.fori_loop(0, chunks, settle_out, 0)


def on_device(
    n_gx, n_gy,
    nest_fields, boundary_strip, strip_owner, terrain_slope, column_metric, relax_rate,
    parent_state, intersection_cell, intersection_row, intersection_count,
):
    fields, levels, cells_x, width = nest_fields.shape
    cap = intersection_cell.shape[3]
    chunks = levels // CH
    n_rows = fields * levels
    quarters = -(-n_rows // 32)
    pieces = []
    for p in range(PIECES):
        first = quarters * p // PIECES
        count = quarters * (p + 1) // PIECES - first
        pieces.append((first, count, min(first * 32, n_rows - count * 32)))
    n_quarter = quarters * 8
    n_half = 2 * n_quarter
    bits = max(n_gx.bit_length() - 3, 1)
    feat = 4 * levels
    feat_pad = -(-(feat + 1) // 128) * 128
    tile = width // 3
    f32 = jnp.float32
    smem = pl.BlockSpec(memory_space=pltpu.SMEM)
    vmem = pl.BlockSpec(memory_space=pltpu.VMEM)
    hbm = pl.BlockSpec(memory_space=pl.ANY)
    dma = pltpu.SemaphoreType.DMA
    out, parent = pl.pallas_call(
        functools.partial(kernel, n_gx, n_gy, cap, tuple(pieces)),
        out_shape=(
            jax.ShapeDtypeStruct((fields, cells_x, levels, width), f32),
            jax.ShapeDtypeStruct((feat, parent_state.shape[1]), f32),
        ),
        in_specs=[smem] * 4 + [hbm] * 6,
        out_specs=(hbm, vmem),
        scratch_shapes=[
            pltpu.VMEM((4, fields, 3, levels + 2 * PAD, width), f32),
            pltpu.VMEM((2, 3, fields, levels, width), f32),
            pltpu.VMEM((2, 3, levels, tile), f32),
            pltpu.VMEM((2, 3, levels, tile), f32),
            pltpu.VMEM((3, 3, 8, width), f32),
            pltpu.VMEM((n_rows, width), f32),
            pltpu.VMEM((n_half, width), f32),
            pltpu.VMEM((n_half, width), f32),
            pltpu.VMEM((n_quarter, width), f32),
            pltpu.VMEM((bits + 1, n_quarter, width), f32),
            pltpu.VMEM((bits, n_quarter, width), f32),
            pltpu.VMEM((n_half, width), f32),
            pltpu.VMEM((n_half, width), f32),
            pltpu.VMEM((n_rows, width), f32),
            pltpu.VMEM((feat_pad, width), f32),
            pltpu.VMEM((n_gy * 8, feat_pad), f32),
            pltpu.VMEM((n_gy * 8, feat_pad), f32),
            pltpu.VMEM((3, 3, width), f32),
            pltpu.VMEM((feat, parent_state.shape[1]), f32),
            dma,
            dma,
            dma((2, 3, chunks)),
            dma((2, 3, chunks)),
            dma((2, 3, chunks)),
            dma((2, 3, chunks)),
            dma((bits + 4, PIECES)),
            dma((bits + 4, PIECES)),
            dma((n_gy,)),
            dma((n_gy,)),
            dma((chunks,)),
            dma((4,)),
            pltpu.VMEM((3, fields, levels, width), f32),
            dma((3, chunks)),
            dma((3, chunks)),
        ],
        compiler_params=pltpu.CompilerParams(
            collective_id=0, has_side_effects=True, vmem_limit_bytes=62 * 1024 * 1024
        ),
    )(
        strip_owner,
        intersection_cell,
        intersection_row,
        intersection_count,
        nest_fields.transpose(0, 2, 1, 3),
        boundary_strip.reshape(n_rows, width),
        terrain_slope,
        column_metric,
        relax_rate,
        parent_state[0].T,
    )
    return out.transpose(0, 2, 1, 3), parent.T[None]


def solution(mesh):
    placed = (
        P(None, None, "gx", "gy"),
        P("gx", None, None, "gy"),
        P(),
        P("gx", "gy"),
        P("gx", "gy"),
        P("gx", "gy"),
        P("gx", "gy", None),
        P("gx", "gy", None, None),
        P("gx", "gy", None, None),
        P("gx", "gy", None),
    )
    return jax.shard_map(
        functools.partial(on_device, mesh.shape["gx"], mesh.shape["gy"]),
        mesh=mesh,
        in_specs=placed,
        out_specs=(P(None, None, "gx", "gy"), P("gx", "gy", None)),
        check_vma=False,
    )
```
